32 devices in a mesh: tm: 8 (over y, x, core), col: 4 (over z).
Axes of the slice: x: 2, y: 2, z: 4, core: 2. Of those that a mesh axis runs over, the one named last changes fastest.
Arguments:
- blocks: float32 [32, 512, 512], P('tm', None, 'col'), as said below
- upper: float32 [32, 512, 512], P('tm', None, 'col'), as said below
- arrow: float32 [32, 64, 512], P('tm', None, 'col'), as said below
- tip: float32 [64, 64], replicated, as said below
- rhs: float32 [32, 512], P('tm'), may hold values from -1 to 1
- rhs_fixed: float32 [64], replicated, may hold values from -6 to 6
Outputs:
- solution: float32 [32, 512], P('tm', 'col')
- solution_fixed: float32 [64], replicated
- mean_log_det: float32 [], replicated
The draws below stay inside these ranges and needn't reach their ends.
Inputs may be any that keep to these rules, and one draw needn't show every extreme that they name: blocks[t] is symmetric for every t, and the matrix Q assembled from blocks, upper, arrow and tip is positive definite. `upper`: Q assembled with these couplings is positive definite. `arrow`: Q assembled with these couplings is positive definite. tip is symmetric, and Q assembled with it is positive definite.
All inputs are finite; a program needn't handle non-finite values.
Results may differ from the reference program's by a relative error of at most 0.0003.
Values sent between devices are 32-bit elements; how exact they have to be, the bound alone decides.
A program may use at most 192 MiB of HBM per device.

```python
import math
import jax
import jax.numpy as jnp
from jax import lax

NODES = 512
EFFECTS = 64
TIMES = 32


def signed_noise(key, shape):
    return jax.random.truncated_normal(key, -4.0, 4.0, shape, jnp.float32)


def log_uniform(key, shape, lowest, highest):
    return jnp.exp(jax.random.uniform(key, shape, jnp.float32, math.log(lowest), math.log(highest)))


def memory_rates(key):
    rate_key = jax.random.fold_in(key, 7005)
    lapse = log_uniform(rate_key, (NODES,), 0.004, 0.06)
    return 1.0 - lapse


def precision_parts(key):
    base_key = jax.random.fold_in(key, 7001)
    mixing_key, scale_key, drift_key = jax.random.split(base_key, 3)
    identity = jnp.eye(NODES, dtype=jnp.float32)
    factors = signed_noise(mixing_key, (TIMES, NODES, NODES))
    spatial = jnp.einsum('tij,tkj->tik', factors, factors, precision=lax.Precision.HIGHEST) / NODES
    spatial = 0.5 * (spatial + jnp.swapaxes(spatial, 1, 2))
    diagonal = log_uniform(scale_key, (TIMES, NODES), 1.0, 2.0)
    spatial = spatial + diagonal[:, :, None] * identity[None]
    rates = memory_rates(key)
    drift_map = rates[None, :, None] * identity[None] + signed_noise(drift_key, (TIMES, NODES, NODES)) * (0.02 / math.sqrt(NODES))
    carried = jnp.einsum('tji,tjk->tik', drift_map, spatial, precision=lax.Precision.HIGHEST)
    return (spatial, drift_map, carried)


def covariate_rows(key):
    return signed_noise(jax.random.fold_in(key, 7003), (TIMES, EFFECTS, NODES)) * (1.5 / math.sqrt(TIMES * NODES))


def draw_blocks(key, part):
    spatial, drift_map, carried = precision_parts(key)
    onward = jnp.einsum('tij,tjk->tik', carried, drift_map, precision=lax.Precision.HIGHEST)
    onward = 0.5 * (onward + jnp.swapaxes(onward, 1, 2))
    onward = jnp.concatenate([onward[1:], jnp.zeros((1, NODES, NODES), jnp.float32)], axis=0)
    nugget_key = jax.random.fold_in(key, 7002)
    nugget = log_uniform(nugget_key, (TIMES, NODES), 0.002, 0.006)
    return spatial + onward + nugget[:, :, None] * jnp.eye(NODES, dtype=jnp.float32)[None]


def draw_upper(key, part):
    spatial, drift_map, carried = precision_parts(key)
    return -carried


def draw_arrow(key, part):
    spatial, drift_map, carried = precision_parts(key)
    covariates = covariate_rows(key)
    direct = jnp.einsum('tej,tjk->tek', covariates, spatial, precision=lax.Precision.HIGHEST)
    lagged = jnp.einsum('tej,tij->tei', covariates, carried, precision=lax.Precision.HIGHEST)
    lagged = jnp.concatenate([lagged[1:], jnp.zeros((1, EFFECTS, NODES), jnp.float32)], axis=0)
    return lagged - direct


def draw_tip(key, part):
    spatial, drift_map, carried = precision_parts(key)
    covariates = covariate_rows(key)
    weighted = jnp.einsum('tej,tjk->tek', covariates, spatial, precision=lax.Precision.HIGHEST)
    loading = jnp.einsum('tek,tfk->ef', weighted, covariates, precision=lax.Precision.HIGHEST)
    loading = 0.5 * (loading + loading.T)
    matrix_key, scale_key = jax.random.split(jax.random.fold_in(key, 404))
    mixing = signed_noise(matrix_key, (EFFECTS, EFFECTS))
    product = jnp.dot(mixing, mixing.T, precision=lax.Precision.HIGHEST) / EFFECTS
    product = 0.5 * (product + product.T)
    diagonal = log_uniform(scale_key, (EFFECTS,), 2.0, 4.0)
    return product + jnp.diag(diagonal) + loading


def draw_rhs(key, part):
    noise_key = jax.random.fold_in(jax.random.fold_in(key, 7004), 0)
    rough_part = signed_noise(noise_key, (TIMES, NODES)) * 0.25
    return rough_part


def centred(stream_key, dims, scale, reach, kind=jnp.bfloat16):
    return jnp.clip(scale * jax.random.normal(stream_key, dims, jnp.float32), -reach, reach).astype(kind)


def setup_inputs(seed: int = 0) -> dict:
    streams_of = jax.random.split(jax.random.key(seed), 7)
    return {
        "blocks": draw_blocks(jax.random.fold_in(streams_of[6], 71), 0),
        "upper": draw_upper(jax.random.fold_in(streams_of[6], 71), 0),
        "arrow": draw_arrow(jax.random.fold_in(streams_of[6], 71), 0),
        "tip": draw_tip(jax.random.fold_in(streams_of[6], 71), 0),
        "rhs": draw_rhs(jax.random.fold_in(streams_of[6], 71), 0),
        "rhs_fixed": centred(streams_of[5], (EFFECTS,), 1.0, 6.0, jnp.float32),
    }


def lower_solve(factor, right_side):
    return lax.linalg.triangular_solve(factor, right_side, left_side=True, lower=True)

def upper_solve(factor, right_side):
    return lax.linalg.triangular_solve(factor, right_side, left_side=True, lower=True, transpose_a=True)

def cross_product(first_operand, second_operand):
    return lax.dot_general(first_operand.astype(jnp.float32), second_operand.astype(jnp.float32), (((0,), (0,)), ((), ())), precision=lax.Precision.HIGHEST, preferred_element_type=jnp.float32)

def apply_matrix(matrix, vector):
    return jnp.dot(matrix.astype(jnp.float32), vector.astype(jnp.float32), precision=lax.Precision.HIGHEST, preferred_element_type=jnp.float32)

def reference(blocks, upper, arrow, tip, rhs, rhs_fixed):
    step_ids = jnp.arange(TIMES, dtype=jnp.int32)

    def forward(carry, inputs):
        factor_prev, side_prev, right_prev, tip_sum, fixed_sum, log_sum = carry
        block, coupling, side_block, right_block, step_id = inputs
        coupled = lower_solve(factor_prev, coupling) * (step_id > 0).astype(jnp.float32)
        factor = jnp.linalg.cholesky(block - cross_product(coupled, coupled))
        side_solved = lower_solve(factor, side_block.T - cross_product(coupled, side_prev))
        right_solved = lower_solve(factor, (right_block - cross_product(coupled, right_prev))[:, None])[:, 0]
        tip_sum = tip_sum + cross_product(side_solved, side_solved)
        fixed_sum = fixed_sum + cross_product(side_solved, right_solved)
        log_sum = log_sum + 2.0 * jnp.sum(jnp.log(jnp.diagonal(factor)))
        return ((factor, side_solved, right_solved, tip_sum, fixed_sum, log_sum), (factor, coupled, side_solved, right_solved))
    initial = (jnp.eye(NODES, dtype=jnp.float32), jnp.zeros((NODES, EFFECTS), jnp.float32), jnp.zeros((NODES,), jnp.float32), jnp.zeros((EFFECTS, EFFECTS), jnp.float32), jnp.zeros((EFFECTS,), jnp.float32), jnp.zeros((), jnp.float32))
    final_carry, stacked = lax.scan(forward, initial, (blocks, upper, arrow, rhs, step_ids))
    tip_sum, fixed_sum, log_sum = (final_carry[3], final_carry[4], final_carry[5])
    factors, couplings, sides, rights = stacked
    fixed_factor = jnp.linalg.cholesky(tip - tip_sum)
    fixed_solved = lower_solve(fixed_factor, (rhs_fixed - fixed_sum)[:, None])
    solution_fixed = upper_solve(fixed_factor, fixed_solved)[:, 0]
    log_total = log_sum + 2.0 * jnp.sum(jnp.log(jnp.diagonal(fixed_factor)))
    next_couplings = jnp.concatenate([couplings[1:], jnp.zeros((1, NODES, NODES), jnp.float32)], axis=0)

    def backward(following, inputs):
        factor, coupling_next, side_solved, right_solved = inputs
        terms = apply_matrix(coupling_next, following) + apply_matrix(side_solved, solution_fixed)
        value = upper_solve(factor, (right_solved - terms)[:, None])[:, 0]
        return (value, value)
    last_value, solution = lax.scan(backward, jnp.zeros((NODES,), jnp.float32), (factors, next_couplings, sides, rights), reverse=True)
    return (solution, solution_fixed, log_total / (TIMES * NODES + EFFECTS))
```

```python
import functools

import jax
import jax.numpy as jnp
from jax import lax
from jax.experimental import pallas as pl
from jax.experimental.pallas import tpu as pltpu
from jax.sharding import PartitionSpec as P


def shifted(block, axis, distance):
    devices = range(lax.axis_size(axis))
    route = [(i - distance, i) for i in devices if i - distance in devices]
    return lax.ppermute(block, axis, route)


def broadcast(x, axis, root):
    mine = lax.axis_index(axis) == root
    return lax.psum(jnp.where(mine, x, jnp.zeros_like(x)), axis)


def lower_solve(inverse, right_side):
    return lax.dot_general(
        inverse,
        right_side,
        (((1,), (0,)), ((), ())),
        precision=lax.Precision.HIGHEST,
        preferred_element_type=jnp.float32,
    )


def upper_solve(inverse, right_side):
    return cross_product(inverse, right_side)


def cross_product(first_operand, second_operand):
    return lax.dot_general(
        first_operand,
        second_operand,
        (((0,), (0,)), ((), ())),
        precision=lax.Precision.HIGHEST,
        preferred_element_type=jnp.float32,
    )


def apply_matrix(matrix, vector):
    return jnp.dot(
        matrix, vector, precision=lax.Precision.HIGHEST, preferred_element_type=jnp.float32
    )


def eliminate_tile(tile_ref):
    side = tile_ref.shape[0]
    rows = lax.broadcasted_iota(jnp.int32, (8, side), 0)
    cols = lax.broadcasted_iota(jnp.int32, (8, side), 1)
    for start in range(0, side, 8):
        strip = tile_ref[start : start + 8, :]
        entry = {}
        for j in range(8):
            spread = jnp.broadcast_to(strip[:, start + j : start + j + 1], (8, side))
            for i in range(j + 1):
                entry[i, j] = jnp.broadcast_to(spread[i : i + 1, :], (8, side))
        inside = (cols >= start) & (cols < start + 8)
        marked = jnp.where(inside, (cols - start == rows).astype(jnp.float32), strip)
        solved = jnp.zeros((8, side), jnp.float32)
        lines = [jnp.broadcast_to(marked[i : i + 1, :], (8, side)) for i in range(8)]
        for i in range(8):
            pivot = entry[i, i]
            scale = lax.rsqrt(pivot)
            scale = scale * (1.5 - 0.5 * (pivot * scale) * scale)
            line = lines[i] * scale
            solved = jnp.where(rows == i, line, solved)
            factor = {j: entry[i, j] * scale for j in range(i + 1, 8)}
            for j in range(i + 1, 8):
                for l in range(j, 8):
                    entry[j, l] = entry[j, l] - factor[j] * factor[l]
                lines[j] = lines[j] - factor[j] * line
        tile_ref[start : start + 8, :] = solved
        if start + 8 < side:
            update = lax.dot_general(
                solved,
                solved,
                (((0,), (0,)), ((), ())),
                precision=lax.Precision.HIGHEST,
                preferred_element_type=jnp.float32,
            )
            below = tile_ref[start + 8 :, :]
            spot = lax.broadcasted_iota(jnp.int32, below.shape, 1)
            cleared = (spot >= start) & (spot < start + 8)
            tile_ref[start + 8 :, :] = jnp.where(cleared, 0.0, below) - update[start + 8 :, :]


def inverse_factor_kernel(side, matrix_ref, out_ref, tile_ref):
    order = matrix_ref.shape[0]
    count = order // side
    out_ref[...] = matrix_ref[...]

    @pl.loop(0, count)
    def _(step):
        start = pl.multiple_of(step * side, side)
        here = pl.ds(start, side)
        tile_ref[...] = out_ref[here, here]
        eliminate_tile(tile_ref)
        row = lax.broadcasted_iota(jnp.int32, (side, side), 0)
        col = lax.broadcasted_iota(jnp.int32, (side, side), 1)
        inverse = jnp.where(row >= col, tile_ref[...], 0.0)
        out_ref[here, :] = lax.dot_general(
            inverse,
            out_ref[here, :],
            (((1,), (0,)), ((), ())),
            precision=lax.Precision.HIGHEST,
            preferred_element_type=jnp.float32,
        )
        out_ref[here, here] = inverse

        @pl.loop(step + 1, count)
        def _(other):
            there = pl.ds(pl.multiple_of(other * side, side), side)
            out_ref[there, here] = jnp.zeros((side, side), jnp.float32)
            out_ref[there, :] = out_ref[there, :] - lax.dot_general(
                out_ref[here, there],
                out_ref[here, :],
                (((0,), (0,)), ((), ())),
                precision=lax.Precision.HIGHEST,
                preferred_element_type=jnp.float32,
            )

    row = lax.broadcasted_iota(jnp.int32, (order, order), 0)
    col = lax.broadcasted_iota(jnp.int32, (order, order), 1)
    out_ref[...] = jnp.where(row >= col, out_ref[...], 0.0)


def inverse_factor(matrix):
    order = matrix.shape[0]
    side = min(order, 128)
    return pl.pallas_call(
        functools.partial(inverse_factor_kernel, side),
        out_shape=jax.ShapeDtypeStruct((order, order), jnp.float32),
        in_specs=[pl.BlockSpec(memory_space=pltpu.VMEM)],
        out_specs=pl.BlockSpec(memory_space=pltpu.VMEM),
        scratch_shapes=[pltpu.VMEM((side, side), jnp.float32)],
        compiler_params=pltpu.CompilerParams(vmem_limit_bytes=32 * 2**20),
        cost_estimate=pl.CostEstimate(
            flops=order**3, bytes_accessed=8 * order**2, transcendentals=order
        ),
    )(matrix)


def log_pivots(factor):
    return -2.0 * jnp.sum(jnp.log(jnp.diagonal(factor)))


def arrow_solve(factor, side_part, right_part):
    solved = lower_solve(factor, jnp.concatenate([side_part.T, right_part[:, None]], axis=1))
    return (solved[:, :-1], solved[:, -1])


def back_value(factor, right_solved, terms):
    return upper_solve(factor, (right_solved - terms)[:, None])[:, 0]


def transposed_coupling(local_part):
    flipped = local_part.T
    return flipped


def whole_panels(low_local, high_local):
    low_whole, high_whole = (low_local, high_local)
    return (low_whole, high_whole)


def per_device(blocks, upper, arrow, tip, rhs, rhs_fixed):
    step_count, node_count, slab_width = blocks.shape
    effect_count = tip.shape[0]
    part_count = lax.axis_size("tm")
    level_count = part_count.bit_length() - 1
    part_index = lax.axis_index("tm")
    offset = lax.axis_index("col") * slab_width
    zero_value = jnp.zeros((), jnp.float32)
    arrows = lax.all_gather(arrow, "col", axis=2, tiled=True)
    received = lax.all_to_all(upper[0], "col", split_axis=0, concat_axis=1, tiled=True)
    coupling = received.T * (part_index > 0).astype(jnp.float32)
    diagonal = blocks[0]
    side_part = arrows[0]
    right_part = rhs[0]
    sent_diag = jnp.zeros((node_count, slab_width), jnp.float32)
    sent_side = jnp.zeros((effect_count, node_count), jnp.float32)
    sent_right = jnp.zeros((node_count,), jnp.float32)
    inner_tip = jnp.zeros((effect_count, effect_count), jnp.float32)
    inner_fixed = jnp.zeros((effect_count,), jnp.float32)
    inner_log = zero_value
    stored_rows = []
    for step_index in range(step_count - 1):
        whole_diag = lax.all_gather(diagonal, "col", axis=1, tiled=True)
        factor = inverse_factor(whole_diag)
        inner_log = inner_log + log_pivots(factor)
        panels = lower_solve(factor, jnp.concatenate([coupling, upper[step_index + 1]], axis=1))
        fill_local = panels[:, :slab_width]
        next_local = panels[:, slab_width:]
        side_solved, right_solved = arrow_solve(factor, side_part, right_part)
        fill_whole, next_whole = (
            lax.all_gather(fill_local, "col", axis=1, tiled=True),
            lax.all_gather(next_local, "col", axis=1, tiled=True),
        )
        sent_diag = sent_diag + cross_product(fill_whole, fill_local)
        sent_side = sent_side + cross_product(side_solved, fill_whole)
        sent_right = sent_right + cross_product(fill_whole, right_solved)
        inner_tip = inner_tip + cross_product(side_solved, side_solved)
        inner_fixed = inner_fixed + cross_product(side_solved, right_solved)
        diagonal = blocks[step_index + 1] - cross_product(next_whole, next_local)
        coupling = -cross_product(next_whole, fill_local)
        side_part = arrows[step_index + 1] - cross_product(side_solved, next_whole)
        right_part = rhs[step_index + 1] - cross_product(next_whole, right_solved)
        stored_rows.append((factor, fill_whole, next_whole, side_solved, right_solved))
    got_diag, got_side, got_right = shifted((sent_diag, sent_side, sent_right), "tm", -1)
    diagonal = diagonal - got_diag
    side_part = side_part - got_side
    right_part = right_part - got_right
    interior_sums = lax.psum((inner_tip, inner_fixed, inner_log), "tm")
    tree_diag, tree_coupling = (
        lax.all_gather(diagonal, "col", axis=1, tiled=True),
        lax.all_gather(coupling, "col", axis=1, tiled=True),
    )
    carried = (
        jnp.zeros((effect_count, effect_count), jnp.float32),
        jnp.zeros((effect_count,), jnp.float32),
        zero_value,
    )
    for level_index in range(level_count):
        stride = 1 << level_index
        position = (part_index + 1) % (2 * stride)
        staying = position == 0
        from_upper = shifted(transposed_coupling(tree_coupling), "tm", -stride)
        factor = inverse_factor(tree_diag)
        column_count = tree_coupling.shape[1]
        panels = lower_solve(factor, jnp.concatenate([tree_coupling, from_upper], axis=1))
        low_local = panels[:, :column_count]
        high_local = panels[:, column_count:]
        side_solved, right_solved = arrow_solve(factor, side_part, right_part)
        low_whole, high_whole = whole_panels(low_local, high_local)
        own_tip = cross_product(side_solved, side_solved)
        own_fixed = cross_product(side_solved, right_solved)
        own_log = log_pivots(factor)
        downward = (
            cross_product(low_whole, low_local),
            cross_product(side_solved, low_whole),
            cross_product(low_whole, right_solved),
        )
        upward = (
            cross_product(high_whole, high_local),
            -cross_product(high_whole, low_local),
            cross_product(side_solved, high_whole),
            cross_product(high_whole, right_solved),
        )
        upward = upward + (carried[0] + own_tip, carried[1] + own_fixed, carried[2] + own_log)
        from_above = shifted((downward[0], downward[1], downward[2]), "tm", -stride)
        from_below = shifted(upward, "tm", stride)
        tree_diag = tree_diag - from_above[0] - from_below[0]
        tree_coupling = from_below[1]
        side_part = side_part - from_above[1] - from_below[2]
        right_part = right_part - from_above[2] - from_below[3]
        carried = (
            jnp.where(staying, carried[0] + from_below[4], carried[0]),
            jnp.where(staying, carried[1] + from_below[5], carried[1]),
            jnp.where(staying, carried[2] + from_below[6], carried[2]),
        )
    factor = inverse_factor(tree_diag)
    side_solved, right_solved = arrow_solve(factor, side_part, right_part)
    root_tip = cross_product(side_solved, side_solved)
    root_fixed = cross_product(side_solved, right_solved)
    root_log = log_pivots(factor)
    order_total = step_count * part_count * node_count + effect_count
    reduced_tip = tip - interior_sums[0] - carried[0] - root_tip
    reduced_fixed = rhs_fixed - interior_sums[1] - carried[1] - root_fixed
    fixed_factor = inverse_factor(reduced_tip)
    candidate = upper_solve(fixed_factor, lower_solve(fixed_factor, reduced_fixed[:, None]))[:, 0]
    log_candidate = interior_sums[2] + carried[2] + root_log + log_pivots(fixed_factor)
    solution_fixed, log_total = (
        broadcast(candidate, "tm", part_count - 1),
        broadcast(log_candidate, "tm", part_count - 1),
    )
    mean_log_det = log_total / order_total
    boundary_value = back_value(factor, right_solved, apply_matrix(side_solved, solution_fixed))
    prior_value = shifted(boundary_value, "tm", 1)
    solved_rows = [boundary_value]
    following = boundary_value
    for step_index in reversed(range(step_count - 1)):
        factor, fill_whole, next_whole, side_solved, right_solved = stored_rows[step_index]
        terms = (
            apply_matrix(fill_whole, prior_value)
            + apply_matrix(next_whole, following)
            + apply_matrix(side_solved, solution_fixed)
        )
        following = back_value(factor, right_solved, terms)
        solved_rows.insert(0, following)
    whole_rows = jnp.stack(solved_rows)
    solution = lax.dynamic_slice_in_dim(whole_rows, offset, slab_width, 1)
    return (solution, solution_fixed, mean_log_det)


def solution(mesh):
    placed = (
        P("tm", None, "col"),
        P("tm", None, "col"),
        P("tm", None, "col"),
        P(),
        P("tm", None),
        P(),
    )
    return jax.shard_map(
        per_device,
        mesh=mesh,
        in_specs=placed,
        out_specs=(P("tm", "col"), P(), P()),
        check_vma=False,
    )
```
